32 devices in a mesh: dp: 2 (over x), branch: 4 (over z), seq: 4 (over y, core).
Axes of the slice: x: 2, y: 2, z: 4, core: 2. Of those that a mesh axis runs over, the one named last changes fastest.
Arguments:
- qkv: bfloat16 [4, 2, 896, 3, 1536], P('branch', 'dp', 'seq'), may hold values from -5.5 to 5.5, as said below
- grad_base: bfloat16 [2, 896, 2432], P('dp', ('branch', 'seq')), may hold values from -12 to 12
- w_out: bfloat16 [4, 1536, 2432], P('branch', 'seq'), may hold values from -0.15625 to 0.15625
- scale_level: int32 [2], P('dp'), may hold values from 0 to 7
- text_count: int32 [2], P('dp'), may hold values from 96 to 384, as said below
Outputs:
- qkv_grad: bfloat16 [4, 2, 896, 3, 1536], P('branch', 'dp', 'seq')
- w_out_grad: float32 [4, 2432, 1536], P('branch', 'dp', 'seq')
The draws below stay inside these ranges and needn't reach their ends.
Inputs may be any that keep to these rules, and one draw needn't show every extreme that they name: `qkv`: the queries, keys and values are real numbers of order one. `text_count`: some sample has all 384 text slots live in every draw.
All inputs are finite; a program needn't handle non-finite values.
Results may differ from the reference program's by a relative error of at most 0.0064.
Values may be sent and summed in bfloat16 or wider, within the bound.
A program may use at most 64 MiB of HBM per device.

```python
import math
import jax
import jax.numpy as jnp
from jax import lax

D = 2432
DH = 64
LAT = 512
TXT = 384
SCALE_LEVELS = 8
SEQ = 896
HD = 1536
GROUPS = 4
BATCH = 2


def draw_qkv(key, part):
    key = jax.random.fold_in(key, 11)
    key_base = jax.random.fold_in(key, 0)
    full_shape = (GROUPS, BATCH, SEQ, 3, HD)
    values = jnp.clip(jax.random.normal(key_base, full_shape, jnp.float32), -4.5, 4.5)
    return values.astype(jnp.bfloat16)


def draw_text_count(key, part):
    key = jax.random.fold_in(key, 23)
    key_counts, key_chosen = jax.random.split(key, 2)
    counts = jax.random.randint(key_counts, (BATCH,), TXT // 4, TXT + 1)
    chosen = jax.random.randint(key_chosen, (), 0, BATCH)
    return jnp.where(jnp.arange(BATCH) == chosen, TXT, counts).astype(jnp.int32)


def spiked(values, key, source, target, blocks, factor):
    def block_of(dim):
        return (jnp.arange(values.shape[dim]) // (values.shape[dim] // blocks)).reshape((-1,) + (1,) * (values.ndim - 1 - dim))

    one_side = jax.random.permutation(key, blocks)[block_of(target)]
    other_side = (block_of(target) + blocks // 2) % blocks
    return jnp.where((block_of(source) == one_side) | (block_of(source) == other_side), factor * values, values)


def block_scale(rng, shape, cuts, least, high):
    factor_of = 1.0
    for dim, blocks in cuts:
        steps = jax.random.uniform(jax.random.fold_in(jax.random.fold_in(rng, 6), dim), (blocks,), jnp.float32, least / len(cuts), high / len(cuts))
        factor_of = factor_of * jnp.repeat(jnp.exp(steps), shape[dim] // blocks).reshape((-1,) + (1,) * (len(shape) - 1 - dim))
    return factor_of


def bell_draw(key, dims, deviation, bound, cuts=(), kind=jnp.bfloat16):
    values = deviation * jax.random.normal(key, dims, jnp.float32)
    if cuts:
        values = values * block_scale(key, dims, cuts, -0.22, 0.18)
    return jnp.clip(values, -bound, bound).astype(kind)


def gaussian_with(rng, extent, scale, reach, cuts, heavy, dtype=jnp.bfloat16):
    entries = scale * jax.random.normal(rng, extent, jnp.float32)
    if cuts:
        entries = entries * block_scale(rng, extent, cuts, -0.22, 0.18)
    return jnp.clip(spiked(entries, jax.random.fold_in(rng, 3), *heavy), -reach, reach).astype(dtype)


def setup_inputs(seed: int = 0) -> dict:
    streams_of = jax.random.split(jax.random.key(seed), 6)
    qkv = draw_qkv(jax.random.fold_in(streams_of[5], 71), 0)
    grad_base = gaussian_with(streams_of[1], (BATCH, SEQ, D), 2.0, 12.0, ((0, 2), (1, 16)), (0, 2, 2, 2.0))
    w_out = bell_draw(streams_of[2], (GROUPS, HD, D), HD ** -0.5, 0.15625, ((0, 4), (1, 4)))
    scale_level = jax.random.randint(streams_of[3], (BATCH,), 0, SCALE_LEVELS).astype(jnp.int32)
    text_count = draw_text_count(jax.random.fold_in(streams_of[5], 71), 0)
    return {"qkv": qkv, "grad_base": grad_base, "w_out": w_out, "scale_level": scale_level, "text_count": text_count}


def head_grads(queries, keys_h, values_h, out_grad, key_valid):
    inv_root = 1.0 / math.sqrt(queries.shape[-1])
    scores = jnp.dot(queries, keys_h.T, preferred_element_type=jnp.float32) * inv_root
    scores = jnp.where(key_valid[None, :], scores, -jnp.inf)
    row_max = lax.optimization_barrier(jnp.max(scores, axis=1, keepdims=True))
    powers = jnp.exp(scores - row_max)
    probs = powers / lax.optimization_barrier(jnp.sum(powers, axis=1, keepdims=True))
    probs_b = probs.astype(jnp.bfloat16)
    attended = jnp.dot(probs_b, values_h, preferred_element_type=jnp.float32).astype(jnp.bfloat16)
    prob_grad = jnp.dot(out_grad, values_h.T, preferred_element_type=jnp.float32)
    row_dot = lax.optimization_barrier(jnp.sum(probs * prob_grad, axis=1, keepdims=True))
    score_grad = (probs * (prob_grad - row_dot)).astype(jnp.bfloat16)
    query_grad = jnp.dot(score_grad, keys_h, preferred_element_type=jnp.float32) * inv_root
    key_grad = jnp.dot(score_grad.T, queries, preferred_element_type=jnp.float32) * inv_root
    value_grad = jnp.dot(probs_b.T, out_grad, preferred_element_type=jnp.float32)
    return (attended, query_grad, key_grad, value_grad)

def attend(activation, upstream, weight, factor, key_valid):
    token_count = activation.shape[0]
    feature_width = weight.shape[0]
    head_count = feature_width // DH
    out_grad = (jnp.dot(upstream, weight.T, preferred_element_type=jnp.float32) * factor).astype(jnp.bfloat16)

    def split_heads(matrix):
        return matrix.reshape(token_count, head_count, DH).transpose(1, 0, 2)

    def join_heads(matrix):
        return matrix.transpose(1, 0, 2).reshape(token_count, feature_width)

    def one_head(pieces):
        return head_grads(pieces[0], pieces[1], pieces[2], pieces[3], key_valid)
    attended, query_grad, key_grad, value_grad = lax.map(one_head, (split_heads(activation[:, 0]), split_heads(activation[:, 1]), split_heads(activation[:, 2]), split_heads(out_grad)))
    act_grads = jnp.stack([join_heads(query_grad), join_heads(key_grad), join_heads(value_grad)], axis=1).astype(jnp.bfloat16)
    return (act_grads, join_heads(attended))

def reference(qkv, grad_base, w_out, scale_level, text_count):
    levels = jnp.arange(SCALE_LEVELS)
    groups = jnp.arange(GROUPS)
    scale_table = jnp.where(groups[None, :] == 0, jnp.float32(1.0), (levels[:, None] + 2 * groups[None, :]).astype(jnp.float32) / 8.0).astype(jnp.float32)
    factors = scale_table[scale_level]
    positions = jnp.arange(SEQ)

    def per_group(pieces):
        group_acts, weight, column = pieces

        def per_sample(running, sample):
            activation, upstream, factor, live_count = sample
            key_valid = positions < LAT + live_count
            act_grads, attended = attend(activation, upstream, weight, factor, key_valid)
            term = jnp.dot(upstream.T, attended, preferred_element_type=jnp.float32) * factor
            return (running + term, act_grads)
        running, act_grads = lax.scan(per_sample, jnp.zeros((D, HD), jnp.float32), (group_acts, grad_base, column, text_count))
        return (act_grads, running)
    qkv_grad, w_out_grad = lax.map(per_group, (qkv, w_out, factors.T))
    return (qkv_grad, w_out_grad)
```

```python
import functools

import jax
import jax.numpy as jnp
from jax import lax
from jax.experimental import pallas as pl
from jax.experimental.pallas import tpu as pltpu
from jax.sharding import PartitionSpec as P

LAT = 512
MIN_TEXT = 96
F32 = jnp.float32
BF16 = jnp.bfloat16
MESH = pl.DeviceIdType.MESH
NT = (((1,), (1,)), ((), ()))
W = 128


def block_diag(pair):
    row = lax.broadcasted_iota(jnp.int32, pair.shape, 0)
    top = row < 64
    zero = jnp.zeros_like(pair)
    return jnp.concatenate([jnp.where(top, pair, zero), jnp.where(top, zero, pair)], axis=1)


def fold_diag(wide):
    row = lax.broadcasted_iota(jnp.int32, (wide.shape[0], W), 0)
    return jnp.where(row < 64, wide[:, :W], wide[:, W:])


def kernel(
    dp, seq, branch, chunks, tokens,
    x_ref, gb_ref, w_ref, level_ref, count_ref,
    out_ref, wg_ref,
    inb, slots, upc, dot_s, e_s, att32, inv_s, attb, q_t, k_t, v_t, gbuf, acc, partf, part_b, rbuf,
    qs, qr, rs, rr, zs, zr, ys, yr, cs, cr, fs, fr, ds_, dr, own_q, own_r,
):
    me_dp = lax.axis_index("dp")
    me_b = lax.axis_index("branch")
    me = lax.axis_index("seq")
    part = tokens // seq
    width = chunks * W
    nblk = tokens // W
    across = lax.rem(me + 2, seq)
    beside = me + 1 - 2 * lax.rem(me, 2)

    barrier = pltpu.get_barrier_semaphore()
    for d in range(1, branch):
        pl.semaphore_signal(barrier, inc=1, device_id={"branch": lax.rem(me_b + d, branch)}, device_id_type=MESH)
    for d in range(1, seq):
        pl.semaphore_signal(barrier, inc=1, device_id={"seq": lax.rem(me + d, seq)}, device_id_type=MESH)
    for d in range(1, dp):
        pl.semaphore_signal(barrier, inc=1, device_id={"dp": lax.rem(me_dp + d, dp)}, device_id_type=MESH)

    own = me_b * seq + me
    rows = gb_ref.shape[0]
    pad = slots.shape[1]
    mine = jnp.concatenate(
        [gb_ref[...].astype(F32), jnp.zeros((pad - rows, gb_ref.shape[1]), F32)], axis=0
    ).astype(BF16)
    slots[own] = mine
    pl.semaphore_wait(barrier, branch + seq + dp - 3)

    def remote(src, dst, ssem, rsem, axis, index):
        return pltpu.make_async_remote_copy(
            src_ref=src, dst_ref=dst, send_sem=ssem, recv_sem=rsem,
            device_id={axis: index}, device_id_type=MESH,
        )

    def qkv_copy(c, d):
        to = lax.rem(me + d, seq)
        lanes = pl.ds(pl.multiple_of(to * width + c * W, W), W)
        at = pl.ds(pl.multiple_of(me * part, 16), part)
        return remote(x_ref.at[:, :, lanes], inb.at[c, :, at, :], qs.at[c, d - 1], qr.at[c, d - 1], "seq", to)

    def qkv_own(c):
        lanes = pl.ds(pl.multiple_of(me * width + c * W, W), W)
        at = pl.ds(pl.multiple_of(me * part, 16), part)
        return pltpu.make_async_copy(x_ref.at[:, :, lanes], inb.at[c, :, at, :], own_q.at[c])

    def line(d):
        return lax.rem(me_b - d + branch, branch) * seq + me

    def z_copy(d):
        return remote(slots.at[own], slots.at[own], zs.at[d - 1], zr.at[d - 1], "branch", lax.rem(me_b + d, branch))

    def y_copy(d):
        return remote(slots.at[line(d)], slots.at[line(d)], ys.at[d], yr.at[d], "seq", across)

    def c_copy(d):
        return remote(slots.at[line(d)], slots.at[line(d)], cs.at[d], cr.at[d], "seq", beside)

    def f_copy(d):
        k = lax.rem(me_b - d + branch, branch) * seq + across
        return remote(slots.at[k], slots.at[k], fs.at[d], fr.at[d], "seq", beside)

    def ret_copy(c, d):
        to = lax.rem(me + d, seq)
        lanes = pl.ds(pl.multiple_of(me * width + c * W, W), W)
        at = pl.ds(pl.multiple_of(to * part, 16), part)
        return remote(gbuf.at[c, :, at, :], out_ref.at[:, :, lanes], rs.at[c, d - 1], rr.at[c, d - 1], "seq", to)

    def ret_own(c):
        lanes = pl.ds(pl.multiple_of(me * width + c * W, W), W)
        at = pl.ds(pl.multiple_of(me * part, 16), part)
        return pltpu.make_async_copy(gbuf.at[c, :, at, :], out_ref.at[:, :, lanes], own_r.at[c])

    def dp_copy(d):
        return remote(part_b.at[d - 1], rbuf.at[d - 1], ds_.at[d - 1], dr.at[d - 1], "dp", lax.rem(me_dp + d, dp))

    def send_qkv(c):
        for d in (2, 1, 3):
            qkv_copy(c, d).start()
        qkv_own(c).start()

    for d in range(1, branch):
        z_copy(d).start()
    send_qkv(0)
    y_copy(0).start()
    c_copy(0).start()
    send_qkv(1)
    send_qkv(2)

    level = level_ref[0]
    limit = LAT + count_ref[0]
    factor = jnp.where(me_b == 0, jnp.float32(1.0), (level + 2 * me_b).astype(F32) / 8.0)
    safe = LAT + MIN_TEXT
    tail = safe + lax.broadcasted_iota(jnp.int32, (tokens - safe, 2 * W), 0)

    def forward(c):
        for d in range(1, seq):
            qkv_copy(c, d).wait_recv()
        qkv_own(c).wait()
        q_t[c] = (inb[c, 0].astype(F32) * 0.125).T.astype(BF16)
        k_t[c] = inb[c, 1].astype(F32).T.astype(BF16)
        v_t[c] = inb[c, 2].astype(F32).T.astype(BF16)

        def step(i, carry):
            lanes = pl.ds(pl.multiple_of(i * W, W), W)
            wide = pl.ds(pl.multiple_of(i * 2 * W, 2 * W), 2 * W)
            s = jnp.dot(inb[c, 1], block_diag(q_t[c, :, lanes]), preferred_element_type=F32)
            s = jnp.concatenate([s[:safe], jnp.where(tail < limit, s[safe:], -1e30)], axis=0)
            top = jnp.max(s, axis=0, keepdims=True)
            e = jnp.exp(s - top)
            inv = 1.0 / jnp.sum(e, axis=0, keepdims=True)
            eb = e.astype(BF16)
            e_s[c, :, wide] = eb
            o = fold_diag(jnp.dot(v_t[c], eb, preferred_element_type=F32) * inv)
            att32[c, :, lanes] = o
            attb[pl.ds(c * W, W), lanes] = o.astype(BF16)
            inv_s[c, :, lanes] = fold_diag(jnp.broadcast_to(inv, (W, 2 * W)))
            return carry

        lax.fori_loop(0, nblk, step, 0)

    def backward(c):
        acc[...] = jnp.zeros_like(acc)

        def step(i, carry):
            lanes = pl.ds(pl.multiple_of(i * W, W), W)
            wide = pl.ds(pl.multiple_of(i * 2 * W, 2 * W), 2 * W)
            do = (dot_s[pl.ds(c * W, W), lanes] * inv_s[c, :, lanes]).astype(BF16)
            prod = do.astype(F32) * att32[c, :, lanes]
            delta = jnp.concatenate(
                [jnp.sum(prod[:64], axis=0, keepdims=True), jnp.sum(prod[64:], axis=0, keepdims=True)], axis=1
            )
            bd = block_diag(do)
            dpr = jnp.dot(inb[c, 2], bd, preferred_element_type=F32)
            eb = e_s[c, :, wide]
            ds = (eb.astype(F32) * (dpr - delta)).astype(BF16)
            acc[1] += lax.dot_general(eb, bd, NT, preferred_element_type=F32)
            acc[0] += lax.dot_general(ds, block_diag(q_t[c, :, lanes]), NT, preferred_element_type=F32)
            dq = fold_diag(jnp.dot(k_t[c], ds, preferred_element_type=F32)) * 0.125
            gbuf[c, 0, lanes, :] = dq.T.astype(BF16)
            return carry

        lax.fori_loop(0, nblk, step, 0)
        gbuf[c, 1] = acc[0].astype(BF16)
        gbuf[c, 2] = acc[1].astype(BF16)
        for d in (2, 1, 3):
            ret_copy(c, d).start()
        ret_own(c).start()

    def relay(d):
        z_copy(d).wait_recv()
        y_copy(d).start()
        c_copy(d).start()

    forward(0)
    for d in range(1, branch):
        relay(d)
    y_copy(0).wait_recv()
    f_copy(0).start()
    forward(1)
    for d in range(1, branch):
        y_copy(d).wait_recv()
        f_copy(d).start()
    forward(2)
    for d in range(branch):
        c_copy(d).wait_recv()
        f_copy(d).wait_recv()

    for b in range(branch):
        whole = jnp.concatenate([slots[b * seq + j].astype(F32)[:rows] for j in range(seq)], axis=0)
        upc[b * seq * rows:(b + 1) * seq * rows, :] = whole.astype(BF16)

    for at in range(0, tokens, 2 * W):
        size = min(2 * W, tokens - at)
        dot_s[:, at:at + size] = factor * lax.dot_general(
            w_ref[...], upc[at:at + size, :], NT, preferred_element_type=F32
        )

    backward(0)

    def weight_step(j, carry):
        lanes = pl.ds(pl.multiple_of(j * W, W), W)
        r = jnp.dot(attb[...], upc[:, lanes], preferred_element_type=F32)
        partf[lanes, :] = r.T * factor
        return carry

    lax.fori_loop(0, upc.shape[1] // W, weight_step, 0)
    share = wg_ref.shape[0]
    for d in range(1, dp):
        to = lax.rem(me_dp + d, dp)
        part_b[d - 1] = partf[pl.ds(pl.multiple_of(to * share, 8), share), :].astype(BF16)
        dp_copy(d).start()

    for c in range(1, chunks):
        backward(c)

    total = partf[pl.ds(pl.multiple_of(me_dp * share, 8), share), :]
    for d in range(1, dp):
        dp_copy(d).wait_recv()
        total = total + rbuf[d - 1].astype(F32)
    wg_ref[...] = total

    for c in range(chunks):
        ret_own(c).wait()
        for d in range(1, seq):
            ret_copy(c, d).wait_recv()
            ret_copy(c, d).wait_send()
            qkv_copy(c, d).wait_send()
    for d in range(1, branch):
        z_copy(d).wait_send()
    for d in range(branch):
        y_copy(d).wait_send()
        c_copy(d).wait_send()
        f_copy(d).wait_send()
    for d in range(1, dp):
        dp_copy(d).wait_send()


def body(dp, seq, branch, qkv, grad_base, w_out, scale_level, text_count):
    part, _, features = qkv.shape[2:]
    tokens = part * seq
    width = features // seq
    chunks = width // W
    rows, model = grad_base.shape[1:]
    pad = -(-rows // 16) * 16
    share = model // dp
    dma = pltpu.SemaphoreType.DMA
    vm = pltpu.VMEM
    vspec = pl.BlockSpec(memory_space=pltpu.VMEM)
    sspec = pl.BlockSpec(memory_space=pltpu.SMEM)
    anyspec = pl.BlockSpec(memory_space=pl.ANY)
    grads, weight_grad = pl.pallas_call(
        functools.partial(kernel, dp, seq, branch, chunks, tokens),
        out_shape=(
            jax.ShapeDtypeStruct((3, part, features), BF16),
            jax.ShapeDtypeStruct((share, width), F32),
        ),
        in_specs=[anyspec, vspec, vspec, sspec, sspec],
        out_specs=(anyspec, vspec),
        scratch_shapes=[
            vm((chunks, 3, tokens, W), BF16),
            vm((branch * seq, pad, model), BF16),
            vm((tokens, model), BF16),
            vm((width, tokens), F32),
            vm((chunks, tokens, 2 * tokens), BF16),
            vm((chunks, W, tokens), F32),
            vm((chunks, W, tokens), F32),
            vm((width, tokens), BF16),
            vm((chunks, W, tokens), BF16),
            vm((chunks, W, tokens), BF16),
            vm((chunks, W, tokens), BF16),
            vm((chunks, 3, tokens, W), BF16),
            vm((2, tokens, W), F32),
            vm((model, width), F32),
            vm((dp - 1, share, width), BF16),
            vm((dp - 1, share, width), BF16),
            dma((chunks, seq - 1)), dma((chunks, seq - 1)),
            dma((chunks, seq - 1)), dma((chunks, seq - 1)),
            dma((branch - 1,)), dma((branch - 1,)),
            dma((branch,)), dma((branch,)),
            dma((branch,)), dma((branch,)),
            dma((branch,)), dma((branch,)),
            dma((dp - 1,)), dma((dp - 1,)),
            dma((chunks,)), dma((chunks,)),
        ],
        compiler_params=pltpu.CompilerParams(
            collective_id=0, has_side_effects=True, vmem_limit_bytes=58 * 1024 * 1024
        ),
    )(jnp.transpose(qkv[0, 0], (1, 0, 2)), grad_base[0], w_out[0], scale_level, text_count)
    return (jnp.transpose(grads, (1, 0, 2))[None, None], weight_grad[None])


def solution(mesh):
    sizes = mesh.shape
    in_specs = (
        P("branch", "dp", "seq", None, None),
        P("dp", ("branch", "seq"), None),
        P("branch", "seq", None),
        P("dp"),
        P("dp"),
    )
    out_specs = (P("branch", "dp", "seq", None, None), P("branch", "dp", "seq"))
    run = functools.partial(body, sizes["dp"], sizes["seq"], sizes["branch"])
    return jax.shard_map(run, mesh=mesh, in_specs=in_specs, out_specs=out_specs, check_vma=False)
```

```python
import functools

import jax
import jax.numpy as jnp
from jax import lax
from jax.experimental import pallas as pl
from jax.experimental.pallas import tpu as pltpu
from jax.sharding import PartitionSpec as P

LAT = 512
MIN_TEXT = 96
F32 = jnp.float32
BF16 = jnp.bfloat16
MESH = pl.DeviceIdType.MESH
NT = (((1,), (1,)), ((), ()))
W = 128


def block_diag(pair):
    row = lax.broadcasted_iota(jnp.int32, pair.shape, 0)
    top = row < 64
    zero = jnp.zeros_like(pair)
    return jnp.concatenate([jnp.where(top, pair, zero), jnp.where(top, zero, pair)], axis=1)


def fold_diag(wide):
    row = lax.broadcasted_iota(jnp.int32, (wide.shape[0], W), 0)
    return jnp.where(row < 64, wide[:, :W], wide[:, W:])


def kernel(
    dp, seq, branch, chunks, tokens,
    x_ref, gb_ref, w_ref, level_ref, count_ref,
    out_ref, wg_ref,
    inb, slots, up, up_t, grad_s, dot_s, e_s, att32, inv_s, q_t, k_t, v_t, gbuf, acc, partf, part_b, rbuf,
    qs, qr, rs, rr, zs, zr, ys, yr, cs, cr, fs, fr, ds_, dr, own_q, own_r,
):
    me_dp = lax.axis_index("dp")
    me_b = lax.axis_index("branch")
    me = lax.axis_index("seq")
    part = tokens // seq
    width = chunks * W
    nblk = tokens // W
    across = lax.rem(me + 2, seq)
    beside = me + 1 - 2 * lax.rem(me, 2)

    barrier = pltpu.get_barrier_semaphore()
    for d in range(1, branch):
        pl.semaphore_signal(barrier, inc=1, device_id={"branch": lax.rem(me_b + d, branch)}, device_id_type=MESH)
    for d in range(1, seq):
        pl.semaphore_signal(barrier, inc=1, device_id={"seq": lax.rem(me + d, seq)}, device_id_type=MESH)
    for d in range(1, dp):
        pl.semaphore_signal(barrier, inc=1, device_id={"dp": lax.rem(me_dp + d, dp)}, device_id_type=MESH)

    own = me_b * seq + me
    rows, model = gb_ref.shape
    full = rows // 16
    half = (slots.shape[2] - full * model)
    last = gb_ref[...].astype(F32)[full * 16:]
    filler = jnp.zeros((8, 2 * half - model), F32)
    last = jnp.concatenate([last[:, :half], jnp.concatenate([last[:, half:], filler], axis=1)], axis=0)
    for i in range(full):
        slots[own, :, i * model:(i + 1) * model] = gb_ref[i * 16:(i + 1) * 16, :]
    slots[own, :, full * model:] = last.astype(BF16)
    pl.semaphore_wait(barrier, branch + seq + dp - 3)

    def remote(src, dst, ssem, rsem, axis, index):
        return pltpu.make_async_remote_copy(
            src_ref=src, dst_ref=dst, send_sem=ssem, recv_sem=rsem,
            device_id={axis: index}, device_id_type=MESH,
        )

    def qkv_copy(c, d):
        to = lax.rem(me + d, seq)
        lanes = pl.ds(pl.multiple_of(to * width + c * W, W), W)
        at = pl.ds(pl.multiple_of(me * part, 16), part)
        return remote(x_ref.at[:, :, lanes], inb.at[c, :, at, :], qs.at[c, d - 1], qr.at[c, d - 1], "seq", to)

    def qkv_own(c):
        lanes = pl.ds(pl.multiple_of(me * width + c * W, W), W)
        at = pl.ds(pl.multiple_of(me * part, 16), part)
        return pltpu.make_async_copy(x_ref.at[:, :, lanes], inb.at[c, :, at, :], own_q.at[c])

    def line(d):
        return lax.rem(me_b - d + branch, branch) * seq + me

    def z_copy(d):
        return remote(slots.at[own], slots.at[own], zs.at[d - 1], zr.at[d - 1], "branch", lax.rem(me_b + d, branch))

    def y_copy(d):
        return remote(slots.at[line(d)], slots.at[line(d)], ys.at[d], yr.at[d], "seq", across)

    def c_copy(d):
        return remote(slots.at[line(d)], slots.at[line(d)], cs.at[d], cr.at[d], "seq", beside)

    def f_copy(d):
        k = lax.rem(me_b - d + branch, branch) * seq + across
        return remote(slots.at[k], slots.at[k], fs.at[d], fr.at[d], "seq", beside)

    def ret_copy(c, d):
        to = lax.rem(me + d, seq)
        lanes = pl.ds(pl.multiple_of(me * width + c * W, W), W)
        at = pl.ds(pl.multiple_of(to * part, 16), part)
        return remote(gbuf.at[c, :, at, :], out_ref.at[:, :, lanes], rs.at[c, d - 1], rr.at[c, d - 1], "seq", to)

    def ret_own(c):
        lanes = pl.ds(pl.multiple_of(me * width + c * W, W), W)
        at = pl.ds(pl.multiple_of(me * part, 16), part)
        return pltpu.make_async_copy(gbuf.at[c, :, at, :], out_ref.at[:, :, lanes], own_r.at[c])

    def dp_copy(c, d):
        to = lax.rem(me_dp + d, dp)
        return remote(part_b.at[d - 1, c], rbuf.at[d - 1, c], ds_.at[d - 1, c], dr.at[d - 1, c], "dp", to)

    def send_qkv(c):
        for d in (2, 1, 3):
            qkv_copy(c, d).start()
        qkv_own(c).start()

    for d in range(1, branch):
        z_copy(d).start()
    send_qkv(0)
    y_copy(0).start()
    c_copy(0).start()

    level = level_ref[0]
    limit = LAT + count_ref[0]
    factor = jnp.where(me_b == 0, jnp.float32(1.0), (level + 2 * me_b).astype(F32) / 8.0)
    safe = LAT + MIN_TEXT
    tail = safe + lax.broadcasted_iota(jnp.int32, (tokens - safe, 2 * W), 0)

    def forward(c):
        for d in range(1, seq):
            qkv_copy(c, d).wait_recv()
        qkv_own(c).wait()
        if 0 < c < chunks - 1:
            send_qkv(c + 1)
        q_t[c] = (inb[c, 0].astype(F32) * 0.125).T.astype(BF16)
        k_t[c] = inb[c, 1].astype(F32).T.astype(BF16)
        v_t[c] = inb[c, 2].astype(F32).T.astype(BF16)

        def step(i, carry):
            lanes = pl.ds(pl.multiple_of(i * W, W), W)
            wide = pl.ds(pl.multiple_of(i * 2 * W, 2 * W), 2 * W)
            s = jnp.dot(inb[c, 1], block_diag(q_t[c, :, lanes]), preferred_element_type=F32)
            s = jnp.concatenate([s[:safe], jnp.where(tail < limit, s[safe:], -1e30)], axis=0)
            top = jnp.max(s, axis=0, keepdims=True)
            e = jnp.exp(s - top)
            inv = 1.0 / jnp.sum(e, axis=0, keepdims=True)
            eb = e.astype(BF16)
            e_s[c, :, wide] = eb
            o = fold_diag(jnp.dot(v_t[c], eb, preferred_element_type=F32) * inv)
            att32[c, :, lanes] = o
            inv_s[c, :, lanes] = fold_diag(jnp.broadcast_to(inv, (W, 2 * W)))
            return carry

        lax.fori_loop(0, nblk, step, 0)

    def backward(c):
        acc[...] = jnp.zeros_like(acc)
        dot_s[...] = grad_s[:, c * W:(c + 1) * W].T

        def step(i, carry):
            lanes = pl.ds(pl.multiple_of(i * W, W), W)
            wide = pl.ds(pl.multiple_of(i * 2 * W, 2 * W), 2 * W)
            do = (dot_s[:, lanes] * inv_s[c, :, lanes]).astype(BF16)
            prod = do.astype(F32) * att32[c, :, lanes]
            delta = jnp.concatenate(
                [jnp.sum(prod[:64], axis=0, keepdims=True), jnp.sum(prod[64:], axis=0, keepdims=True)], axis=1
            )
            bd = block_diag(do)
            dpr = jnp.dot(inb[c, 2], bd, preferred_element_type=F32)
            eb = e_s[c, :, wide]
            ds = (eb.astype(F32) * (dpr - delta)).astype(BF16)
            acc[1] += lax.dot_general(eb, bd, NT, preferred_element_type=F32)
            acc[0] += lax.dot_general(ds, block_diag(q_t[c, :, lanes]), NT, preferred_element_type=F32)
            dq = fold_diag(jnp.dot(k_t[c], ds, preferred_element_type=F32)) * 0.125
            gbuf[c, 0, lanes, :] = dq.T.astype(BF16)
            return carry

        lax.fori_loop(0, nblk, step, 0)
        gbuf[c, 1] = acc[0].astype(BF16)
        gbuf[c, 2] = acc[1].astype(BF16)
        for d in (2, 1, 3):
            ret_copy(c, d).start()
        ret_own(c).start()

    def relay(d):
        z_copy(d).wait_recv()
        y_copy(d).start()
        c_copy(d).start()

    def quarter(d):
        c_copy(d).wait_recv()
        f_copy(d).wait_recv()
        b = lax.rem(me_b - d + branch, branch)
        pieces = []
        for j in range(seq):
            block = slots[b * seq + j].astype(F32)
            pieces += [block[:, i * model:(i + 1) * model] for i in range(full)]
            rest = block[:, full * model:]
            pieces.append(jnp.concatenate([rest[:8], rest[8:, :model - half]], axis=1))
        pieces.append(jnp.zeros((up.shape[1] - part, model), F32))
        up[b] = jnp.concatenate(pieces, axis=0).astype(BF16)
        at = pl.ds(pl.multiple_of(b * part, 16), part)
        grad_s[at, :] = factor * lax.dot_general(up[b, :part, :], w_ref[...], NT, preferred_element_type=F32)

    def turn(d):
        b = lax.rem(me_b - d + branch, branch)
        up_t[b] = up[b].T

    def weight(c):
        att = att32[c].astype(BF16)
        fill = jnp.zeros((W, up.shape[1] - part), BF16)
        sum_ = jnp.zeros((model, W), F32)
        for b in range(branch):
            att_b = jnp.concatenate([att[:, b * part:(b + 1) * part], fill], axis=1)
            sum_ = sum_ + lax.dot_general(up_t[b], att_b, NT, preferred_element_type=F32)
        partf[c] = sum_ * factor
        for d in range(1, dp):
            to = lax.rem(me_dp + d, dp)
            part_b[d - 1, c] = partf[c, pl.ds(pl.multiple_of(to * share, 8), share), :].astype(BF16)
            dp_copy(c, d).start()

    share = wg_ref.shape[0]
    forward(0)
    y_copy(0).wait_recv()
    f_copy(0).start()
    relay(1)
    quarter(0)
    relay(2)
    y_copy(1).wait_recv()
    f_copy(1).start()
    relay(3)
    send_qkv(1)
    turn(0)
    quarter(1)
    turn(1)
    for d in range(2, branch):
        y_copy(d).wait_recv()
        f_copy(d).start()
        quarter(d)
        if d < branch - 1:
            turn(d)
    backward(0)
    turn(branch - 1)
    weight(0)
    for c in range(1, chunks):
        forward(c)
        backward(c)
        weight(c)

    for c in range(chunks):
        total = partf[c, pl.ds(pl.multiple_of(me_dp * share, 8), share), :]
        for d in range(1, dp):
            dp_copy(c, d).wait_recv()
            total = total + rbuf[d - 1, c].astype(F32)
        wg_ref[:, c * W:(c + 1) * W] = total

    for c in range(chunks):
        ret_own(c).wait()
        for d in range(1, seq):
            ret_copy(c, d).wait_recv()
            ret_copy(c, d).wait_send()
            qkv_copy(c, d).wait_send()
    for d in range(1, branch):
        z_copy(d).wait_send()
    for d in range(branch):
        y_copy(d).wait_send()
        c_copy(d).wait_send()
        f_copy(d).wait_send()
    for d in range(1, dp):
        for c in range(chunks):
            dp_copy(c, d).wait_send()


def body(dp, seq, branch, qkv, grad_base, w_out, scale_level, text_count):
    part, _, features = qkv.shape[2:]
    tokens = part * seq
    width = features // seq
    chunks = width // W
    rows, model = grad_base.shape[1:]
    tiles = rows // 8 * (model // W)
    packed = (tiles + tiles % 2) // 2 * W
    group = -(-part // W) * W
    share = model // dp
    dma = pltpu.SemaphoreType.DMA
    vm = pltpu.VMEM
    vspec = pl.BlockSpec(memory_space=pltpu.VMEM)
    sspec = pl.BlockSpec(memory_space=pltpu.SMEM)
    anyspec = pl.BlockSpec(memory_space=pl.ANY)
    grads, weight_grad = pl.pallas_call(
        functools.partial(kernel, dp, seq, branch, chunks, tokens),
        out_shape=(
            jax.ShapeDtypeStruct((3, part, features), BF16),
            jax.ShapeDtypeStruct((share, width), F32),
        ),
        in_specs=[anyspec, vspec, vspec, sspec, sspec],
        out_specs=(anyspec, vspec),
        scratch_shapes=[
            vm((chunks, 3, tokens, W), BF16),
            vm((branch * seq, 16, packed), BF16),
            vm((branch, group, model), BF16),
            vm((branch, model, group), BF16),
            vm((tokens, width), F32),
            vm((W, tokens), F32),
            vm((chunks, tokens, 2 * tokens), BF16),
            vm((chunks, W, tokens), F32),
            vm((chunks, W, tokens), F32),
            vm((chunks, W, tokens), BF16),
            vm((chunks, W, tokens), BF16),
            vm((chunks, W, tokens), BF16),
            vm((chunks, 3, tokens, W), BF16),
            vm((2, tokens, W), F32),
            vm((chunks, model, W), F32),
            vm((dp - 1, chunks, share, W), BF16),
            vm((dp - 1, chunks, share, W), BF16),
            dma((chunks, seq - 1)), dma((chunks, seq - 1)),
            dma((chunks, seq - 1)), dma((chunks, seq - 1)),
            dma((branch - 1,)), dma((branch - 1,)),
            dma((branch,)), dma((branch,)),
            dma((branch,)), dma((branch,)),
            dma((branch,)), dma((branch,)),
            dma((dp - 1, chunks)), dma((dp - 1, chunks)),
            dma((chunks,)), dma((chunks,)),
        ],
        compiler_params=pltpu.CompilerParams(
            collective_id=0, has_side_effects=True, vmem_limit_bytes=58 * 1024 * 1024
        ),
    )(jnp.transpose(qkv[0, 0], (1, 0, 2)), grad_base[0], w_out[0], scale_level, text_count)
    return (jnp.transpose(grads, (1, 0, 2))[None, None], weight_grad[None])


def solution(mesh):
    sizes = mesh.shape
    in_specs = (
        P("branch", "dp", "seq", None, None),
        P("dp", ("branch", "seq"), None),
        P("branch", "seq", None),
        P("dp"),
        P("dp"),
    )
    out_specs = (P("branch", "dp", "seq", None, None), P("branch", "dp", "seq"))
    run = functools.partial(body, sizes["dp"], sizes["seq"], sizes["branch"])
    return jax.shard_map(run, mesh=mesh, in_specs=in_specs, out_specs=out_specs, check_vma=False)
```

```python
import functools

import jax
import jax.numpy as jnp
from jax import lax
from jax.experimental import pallas as pl
from jax.experimental.pallas import tpu as pltpu
from jax.sharding import PartitionSpec as P

LAT = 512
MIN_TEXT = 96
F32 = jnp.float32
BF16 = jnp.bfloat16
MESH = pl.DeviceIdType.MESH
NT = (((1,), (1,)), ((), ()))
W = 128


def block_diag(pair):
    row = lax.broadcasted_iota(jnp.int32, pair.shape, 0)
    top = row < 64
    zero = jnp.zeros_like(pair)
    return jnp.concatenate([jnp.where(top, pair, zero), jnp.where(top, zero, pair)], axis=1)


def fold_diag(wide):
    row = lax.broadcasted_iota(jnp.int32, (wide.shape[0], W), 0)
    return jnp.where(row < 64, wide[:, :W], wide[:, W:])


def kernel(
    dp, seq, branch, chunks, tokens,
    x_ref, gb_ref, w_ref, level_ref, count_ref,
    out_ref, wg_ref,
    inb, slots, up, up_t, grad_s, do_t, att_t, q_t, k_t, v_t, gbuf, acc, partf, part_b, rbuf,
    qs, qr, rs, rr, zs, zr, ys, yr, cs, cr, fs, fr, ds_, dr, own_q, own_r,
):
    me_dp = lax.axis_index("dp")
    me_b = lax.axis_index("branch")
    me = lax.axis_index("seq")
    part = tokens // seq
    width = chunks * W
    nblk = tokens // W
    across = lax.rem(me + 2, seq)
    beside = me + 1 - 2 * lax.rem(me, 2)

    barrier = pltpu.get_barrier_semaphore()
    for d in range(1, branch):
        pl.semaphore_signal(barrier, inc=1, device_id={"branch": lax.rem(me_b + d, branch)}, device_id_type=MESH)
    for d in range(1, seq):
        pl.semaphore_signal(barrier, inc=1, device_id={"seq": lax.rem(me + d, seq)}, device_id_type=MESH)
    for d in range(1, dp):
        pl.semaphore_signal(barrier, inc=1, device_id={"dp": lax.rem(me_dp + d, dp)}, device_id_type=MESH)

    own = me_b * seq + me
    rows, model = gb_ref.shape
    full = rows // 16
    half = (slots.shape[2] - full * model)
    last = gb_ref[...].astype(F32)[full * 16:]
    filler = jnp.zeros((8, 2 * half - model), F32)
    last = jnp.concatenate([last[:, :half], jnp.concatenate([last[:, half:], filler], axis=1)], axis=0)
    for i in range(full):
        slots[own, :, i * model:(i + 1) * model] = gb_ref[i * 16:(i + 1) * 16, :]
    slots[own, :, full * model:] = last.astype(BF16)
    pl.semaphore_wait(barrier, branch + seq + dp - 3)

    def remote(src, dst, ssem, rsem, axis, index):
        return pltpu.make_async_remote_copy(
            src_ref=src, dst_ref=dst, send_sem=ssem, recv_sem=rsem,
            device_id={axis: index}, device_id_type=MESH,
        )

    def qkv_copy(c, d):
        to = lax.rem(me + d, seq)
        lanes = pl.ds(pl.multiple_of(to * width + c * W, W), W)
        at = pl.ds(pl.multiple_of(me * part, 16), part)
        return remote(x_ref.at[:, :, lanes], inb.at[c, :, at, :], qs.at[c, d - 1], qr.at[c, d - 1], "seq", to)

    def qkv_own(c):
        lanes = pl.ds(pl.multiple_of(me * width + c * W, W), W)
        at = pl.ds(pl.multiple_of(me * part, 16), part)
        return pltpu.make_async_copy(x_ref.at[:, :, lanes], inb.at[c, :, at, :], own_q.at[c])

    def line(d):
        return lax.rem(me_b - d + branch, branch) * seq + me

    def z_copy(d):
        return remote(slots.at[own], slots.at[own], zs.at[d - 1], zr.at[d - 1], "branch", lax.rem(me_b + d, branch))

    def y_copy(d):
        return remote(slots.at[line(d)], slots.at[line(d)], ys.at[d], yr.at[d], "seq", across)

    def c_copy(d):
        return remote(slots.at[line(d)], slots.at[line(d)], cs.at[d], cr.at[d], "seq", beside)

    def f_copy(d):
        k = lax.rem(me_b - d + branch, branch) * seq + across
        return remote(slots.at[k], slots.at[k], fs.at[d], fr.at[d], "seq", beside)

    def ret_copy(c, d):
        to = lax.rem(me + d, seq)
        lanes = pl.ds(pl.multiple_of(me * width + c * W, W), W)
        at = pl.ds(pl.multiple_of(to * part, 16), part)
        return remote(gbuf.at[c, :, at, :], out_ref.at[:, :, lanes], rs.at[c, d - 1], rr.at[c, d - 1], "seq", to)

    def ret_own(c):
        lanes = pl.ds(pl.multiple_of(me * width + c * W, W), W)
        at = pl.ds(pl.multiple_of(me * part, 16), part)
        return pltpu.make_async_copy(gbuf.at[c, :, at, :], out_ref.at[:, :, lanes], own_r.at[c])

    def dp_copy(c, d):
        to = lax.rem(me_dp + d, dp)
        return remote(part_b.at[d - 1, c], rbuf.at[d - 1, c], ds_.at[d - 1, c], dr.at[d - 1, c], "dp", to)

    def send_qkv(c):
        for d in (2, 1, 3):
            qkv_copy(c, d).start()
        qkv_own(c).start()

    z_copy(1).start()
    z_copy(branch - 1).start()
    y_copy(0).start()
    c_copy(0).start()
    send_qkv(0)

    level = level_ref[0]
    limit = LAT + count_ref[0]
    factor = jnp.where(me_b == 0, jnp.float32(1.0), (level + 2 * me_b).astype(F32) / 8.0)
    safe = LAT + MIN_TEXT
    tail = safe + lax.broadcasted_iota(jnp.int32, (tokens - safe, 2 * W), 0)

    def attention(c):
        for d in range(1, seq):
            qkv_copy(c, d).wait_recv()
        qkv_own(c).wait()

        @pl.when(c + 2 < chunks)
        def _():
            send_qkv(c + 2)

        q_t[...] = (inb[c, 0].astype(F32) * 0.125).T.astype(BF16)
        k_t[...] = inb[c, 1].astype(F32).T.astype(BF16)
        v_t[...] = inb[c, 2].astype(F32).T.astype(BF16)
        do_t[...] = grad_s[:, pl.ds(pl.multiple_of(c * W, W), W)].T.astype(BF16)
        acc[...] = jnp.zeros_like(acc)

        for i in range(nblk):
            lanes = slice(i * W, (i + 1) * W)
            do = do_t[:, lanes]
            bdq = block_diag(q_t[:, lanes])
            bdo = block_diag(do)
            s = jnp.dot(inb[c, 1], bdq, preferred_element_type=F32)
            dpr = jnp.dot(inb[c, 2], bdo, preferred_element_type=F32)
            s = jnp.concatenate([s[:safe], jnp.where(tail < limit, s[safe:], -1e30)], axis=0)
            e = jnp.exp(s - jnp.max(s, axis=0, keepdims=True))
            probs = e * (1.0 / jnp.sum(e, axis=0, keepdims=True))
            pb = probs.astype(BF16)
            o = fold_diag(jnp.dot(v_t[...], pb, preferred_element_type=F32))
            att_t[c, :, lanes] = o.astype(BF16)
            prod = do.astype(F32) * o
            delta = jnp.concatenate(
                [jnp.sum(prod[:64], axis=0, keepdims=True), jnp.sum(prod[64:], axis=0, keepdims=True)], axis=1
            )
            acc[1] += lax.dot_general(pb, bdo, NT, preferred_element_type=F32)
            ds = (probs * (dpr - delta)).astype(BF16)
            acc[0] += lax.dot_general(ds, bdq, NT, preferred_element_type=F32)
            dq = fold_diag(jnp.dot(k_t[...], ds, preferred_element_type=F32)) * 0.125
            gbuf[c, 0, lanes, :] = dq.T.astype(BF16)

        gbuf[c, 1] = acc[0].astype(BF16)
        gbuf[c, 2] = acc[1].astype(BF16)
        for d in (2, 1, 3):
            ret_copy(c, d).start()
        ret_own(c).start()

    def relay(d):
        z_copy(d).wait_recv()
        y_copy(d).start()
        c_copy(d).start()

    def quarter(d):
        c_copy(d).wait_recv()
        f_copy(d).wait_recv()
        b = lax.rem(me_b - d + branch, branch)
        pieces = []
        for j in range(seq):
            block = slots[b * seq + j].astype(F32)
            pieces += [block[:, i * model:(i + 1) * model] for i in range(full)]
            rest = block[:, full * model:]
            pieces.append(jnp.concatenate([rest[:8], rest[8:, :model - half]], axis=1))
        pieces.append(jnp.zeros((up.shape[1] - part, model), F32))
        up[b] = jnp.concatenate(pieces, axis=0).astype(BF16)
        at = pl.ds(pl.multiple_of(b * part, 16), part)
        grad_s[at, :] = factor * lax.dot_general(up[b, :part, :], w_ref[...], NT, preferred_element_type=F32)

    def turn(d):
        b = lax.rem(me_b - d + branch, branch)
        up_t[b] = up[b].T

    def weight(c):
        att = att_t[c]
        fill = jnp.zeros((W, up.shape[1] - part), BF16)
        sum_ = jnp.zeros((model, W), F32)
        for b in range(branch):
            att_b = jnp.concatenate([att[:, b * part:(b + 1) * part], fill], axis=1)
            sum_ = sum_ + lax.dot_general(up_t[b], att_b, NT, preferred_element_type=F32)
        partf[c] = sum_ * factor
        for d in range(1, dp):
            to = lax.rem(me_dp + d, dp)
            part_b[d - 1, c] = partf[c, pl.ds(pl.multiple_of(to * share, 8), share), :].astype(BF16)
            dp_copy(c, d).start()

    share = wg_ref.shape[0]
    far = [d for d in range(2, branch - 1)]
    relay(1)
    for d in far:
        z_copy(d).start()
    y_copy(0).wait_recv()
    f_copy(0).start()
    relay(branch - 1)
    quarter(0)
    turn(0)
    y_copy(1).wait_recv()
    f_copy(1).start()
    quarter(1)
    turn(1)
    for d in far:
        relay(d)
    send_qkv(1)
    for d in [branch - 1] + far:
        y_copy(d).wait_recv()
        f_copy(d).start()
        quarter(d)
        turn(d)

    def head_pair(c, carry):
        attention(c)
        weight(c)
        return carry

    lax.fori_loop(0, chunks, head_pair, 0)

    for c in range(chunks):
        total = partf[c, pl.ds(pl.multiple_of(me_dp * share, 8), share), :]
        for d in range(1, dp):
            dp_copy(c, d).wait_recv()
            total = total + rbuf[d - 1, c].astype(F32)
        wg_ref[:, c * W:(c + 1) * W] = total

    for c in range(chunks):
        ret_own(c).wait()
        for d in range(1, seq):
            ret_copy(c, d).wait_recv()
            ret_copy(c, d).wait_send()
            qkv_copy(c, d).wait_send()
    for d in range(1, branch):
        z_copy(d).wait_send()
    for d in range(branch):
        y_copy(d).wait_send()
        c_copy(d).wait_send()
        f_copy(d).wait_send()
    for d in range(1, dp):
        for c in range(chunks):
            dp_copy(c, d).wait_send()


def body(dp, seq, branch, qkv, grad_base, w_out, scale_level, text_count):
    part, _, features = qkv.shape[2:]
    tokens = part * seq
    width = features // seq
    chunks = width // W
    rows, model = grad_base.shape[1:]
    tiles = rows // 8 * (model // W)
    packed = (tiles + tiles % 2) // 2 * W
    group = -(-part // W) * W
    share = model // dp
    dma = pltpu.SemaphoreType.DMA
    vm = pltpu.VMEM
    vspec = pl.BlockSpec(memory_space=pltpu.VMEM)
    sspec = pl.BlockSpec(memory_space=pltpu.SMEM)
    anyspec = pl.BlockSpec(memory_space=pl.ANY)
    grads, weight_grad = pl.pallas_call(
        functools.partial(kernel, dp, seq, branch, chunks, tokens),
        out_shape=(
            jax.ShapeDtypeStruct((3, part, features), BF16),
            jax.ShapeDtypeStruct((share, width), F32),
        ),
        in_specs=[anyspec, vspec, vspec, sspec, sspec],
        out_specs=(anyspec, vspec),
        scratch_shapes=[
            vm((chunks, 3, tokens, W), BF16),
            vm((branch * seq, 16, packed), BF16),
            vm((branch, group, model), BF16),
            vm((branch, model, group), BF16),
            vm((tokens, width), F32),
            vm((W, tokens), BF16),
            vm((chunks, W, tokens), BF16),
            vm((W, tokens), BF16),
            vm((W, tokens), BF16),
            vm((W, tokens), BF16),
            vm((chunks, 3, tokens, W), BF16),
            vm((2, tokens, W), F32),
            vm((chunks, model, W), F32),
            vm((dp - 1, chunks, share, W), BF16),
            vm((dp - 1, chunks, share, W), BF16),
            dma((chunks, seq - 1)), dma((chunks, seq - 1)),
            dma((chunks, seq - 1)), dma((chunks, seq - 1)),
            dma((branch - 1,)), dma((branch - 1,)),
            dma((branch,)), dma((branch,)),
            dma((branch,)), dma((branch,)),
            dma((branch,)), dma((branch,)),
            dma((dp - 1, chunks)), dma((dp - 1, chunks)),
            dma((chunks,)), dma((chunks,)),
        ],
        compiler_params=pltpu.CompilerParams(
            collective_id=0, has_side_effects=True, vmem_limit_bytes=58 * 1024 * 1024
        ),
    )(jnp.transpose(qkv[0, 0], (1, 0, 2)), grad_base[0], w_out[0], scale_level, text_count)
    return (jnp.transpose(grads, (1, 0, 2))[None, None], weight_grad[None])


def solution(mesh):
    sizes = mesh.shape
    in_specs = (
        P("branch", "dp", "seq", None, None),
        P("dp", ("branch", "seq"), None),
        P("branch", "seq", None),
        P("dp"),
        P("dp"),
    )
    out_specs = (P("branch", "dp", "seq", None, None), P("branch", "dp", "seq"))
    run = functools.partial(body, sizes["dp"], sizes["seq"], sizes["branch"])
    return jax.shard_map(run, mesh=mesh, in_specs=in_specs, out_specs=out_specs, check_vma=False)
```

```python
import functools

import jax
import jax.numpy as jnp
from jax import lax
from jax.experimental import pallas as pl
from jax.experimental.pallas import tpu as pltpu
from jax.sharding import PartitionSpec as P

LAT = 512
MIN_TEXT = 96
F32 = jnp.float32
BF16 = jnp.bfloat16
MESH = pl.DeviceIdType.MESH
NT = (((1,), (1,)), ((), ()))
W = 128


def block_diag(pair):
    row = lax.broadcasted_iota(jnp.int32, pair.shape, 0)
    top = row < 64
    zero = jnp.zeros_like(pair)
    return jnp.concatenate([jnp.where(top, pair, zero), jnp.where(top, zero, pair)], axis=1)


def fold_diag(wide):
    row = lax.broadcasted_iota(jnp.int32, (wide.shape[0], W), 0)
    return jnp.where(row < 64, wide[:, :W], wide[:, W:])


def kernel(
    dp, seq, branch, chunks, tokens,
    x_ref, gb_ref, w_ref, level_ref, count_ref,
    out_ref, wg_ref,
    inb, slots, up, up_t, grad_s, do_t, att_t, q_t, k_t, v_t, gbuf, acc, partf, part_b, rbuf,
    qs, qr, rs, rr, zs, zr, bs, br, ys, yr, cs, cr, fs, fr, ds_, dr, own_q, own_r,
):
    me_dp = lax.axis_index("dp")
    me_b = lax.axis_index("branch")
    me = lax.axis_index("seq")
    part = tokens // seq
    width = chunks * W
    nblk = tokens // W
    across = lax.rem(me + 2, seq)
    beside = me + 1 - 2 * lax.rem(me, 2)

    barrier = pltpu.get_barrier_semaphore()
    for d in range(1, branch):
        pl.semaphore_signal(barrier, inc=1, device_id={"branch": lax.rem(me_b + d, branch)}, device_id_type=MESH)
    for d in range(1, seq):
        pl.semaphore_signal(barrier, inc=1, device_id={"seq": lax.rem(me + d, seq)}, device_id_type=MESH)
    for d in range(1, dp):
        pl.semaphore_signal(barrier, inc=1, device_id={"dp": lax.rem(me_dp + d, dp)}, device_id_type=MESH)

    own = me_b * seq + me
    rows, model = gb_ref.shape
    full = rows // 16
    half = (slots.shape[2] - full * model)
    last = gb_ref[...].astype(F32)[full * 16:]
    filler = jnp.zeros((8, 2 * half - model), F32)
    last = jnp.concatenate([last[:, :half], jnp.concatenate([last[:, half:], filler], axis=1)], axis=0)
    for i in range(full):
        slots[own, :, i * model:(i + 1) * model] = gb_ref[i * 16:(i + 1) * 16, :]
    slots[own, :, full * model:] = last.astype(BF16)
    pl.semaphore_wait(barrier, branch + seq + dp - 3)

    def remote(src, dst, ssem, rsem, axis, index):
        return pltpu.make_async_remote_copy(
            src_ref=src, dst_ref=dst, send_sem=ssem, recv_sem=rsem,
            device_id={axis: index}, device_id_type=MESH,
        )

    def qkv_copy(c, d):
        to = lax.rem(me + d, seq)
        lanes = pl.ds(pl.multiple_of(to * width + c * W, W), W)
        at = pl.ds(pl.multiple_of(me * part, 16), part)
        return remote(x_ref.at[:, :, lanes], inb.at[c, :, at, :], qs.at[c, d - 1], qr.at[c, d - 1], "seq", to)

    def qkv_own(c):
        lanes = pl.ds(pl.multiple_of(me * width + c * W, W), W)
        at = pl.ds(pl.multiple_of(me * part, 16), part)
        return pltpu.make_async_copy(x_ref.at[:, :, lanes], inb.at[c, :, at, :], own_q.at[c])

    def line(d):
        return lax.rem(me_b - d + branch, branch) * seq + me

    cut = slots.shape[2] // W // 2 * W
    first, second = slice(0, cut), slice(cut, slots.shape[2])

    def on_line(d):
        if d in (1, branch - 1):
            return 0, lax.rem(me_b + d, branch)
        return d - 1, lax.rem(me_b + 1, branch)

    def z_copy(d):
        back, to = on_line(d)
        block = slots.at[line(back)]
        return remote(block, block, zs.at[d - 1], zr.at[d - 1], "branch", to)

    def b_copy(d):
        back, to = on_line(d)
        k = lax.rem(me_b - back + branch, branch) * seq + across
        block = slots.at[k, :, second]
        return remote(block, block, bs.at[d - 1], br.at[d - 1], "branch", to)

    def y_copy(d):
        block = slots.at[line(d)] if d == 0 else slots.at[line(d), :, first]
        return remote(block, block, ys.at[d], yr.at[d], "seq", across)

    def c_copy(d):
        return remote(slots.at[line(d)], slots.at[line(d)], cs.at[d], cr.at[d], "seq", beside)

    def f_copy(d):
        k = lax.rem(me_b - d + branch, branch) * seq + across
        return remote(slots.at[k], slots.at[k], fs.at[d], fr.at[d], "seq", beside)

    def ret_copy(c, d):
        to = lax.rem(me + d, seq)
        lanes = pl.ds(pl.multiple_of(me * width + c * W, W), W)
        at = pl.ds(pl.multiple_of(to * part, 16), part)
        return remote(gbuf.at[c, :, at, :], out_ref.at[:, :, lanes], rs.at[c, d - 1], rr.at[c, d - 1], "seq", to)

    def ret_own(c):
        lanes = pl.ds(pl.multiple_of(me * width + c * W, W), W)
        at = pl.ds(pl.multiple_of(me * part, 16), part)
        return pltpu.make_async_copy(gbuf.at[c, :, at, :], out_ref.at[:, :, lanes], own_r.at[c])

    def dp_copy(c, d):
        to = lax.rem(me_dp + d, dp)
        return remote(part_b.at[d - 1, c], rbuf.at[d - 1, c], ds_.at[d - 1, c], dr.at[d - 1, c], "dp", to)

    def send_qkv(c):
        for d in (2, 1, 3):
            qkv_copy(c, d).start()
        qkv_own(c).start()

    z_copy(1).start()
    z_copy(branch - 1).start()
    y_copy(0).start()
    c_copy(0).start()
    send_qkv(0)

    level = level_ref[0]
    limit = LAT + count_ref[0]
    factor = jnp.where(me_b == 0, jnp.float32(1.0), (level + 2 * me_b).astype(F32) / 8.0)
    safe = LAT + MIN_TEXT
    tail = safe + lax.broadcasted_iota(jnp.int32, (tokens - safe, 2 * W), 0)

    def attention(c):
        for d in range(1, seq):
            qkv_copy(c, d).wait_recv()
        qkv_own(c).wait()

        @pl.when(c + 2 < chunks)
        def _():
            send_qkv(c + 2)

        q_t[...] = (inb[c, 0].astype(F32) * 0.125).T.astype(BF16)
        k_t[...] = inb[c, 1].astype(F32).T.astype(BF16)
        v_t[...] = inb[c, 2].astype(F32).T.astype(BF16)
        do_t[...] = grad_s[:, pl.ds(pl.multiple_of(c * W, W), W)].T.astype(BF16)
        acc[...] = jnp.zeros_like(acc)

        for i in range(nblk):
            lanes = slice(i * W, (i + 1) * W)
            do = do_t[:, lanes]
            bdq = block_diag(q_t[:, lanes])
            bdo = block_diag(do)
            s = jnp.dot(inb[c, 1], bdq, preferred_element_type=F32)
            dpr = jnp.dot(inb[c, 2], bdo, preferred_element_type=F32)
            s = jnp.concatenate([s[:safe], jnp.where(tail < limit, s[safe:], -1e30)], axis=0)
            e = jnp.exp(s - jnp.max(s, axis=0, keepdims=True))
            probs = e * (1.0 / jnp.sum(e, axis=0, keepdims=True))
            pb = probs.astype(BF16)
            o = fold_diag(jnp.dot(v_t[...], pb, preferred_element_type=F32))
            att_t[c, :, lanes] = o.astype(BF16)
            prod = do.astype(F32) * o
            delta = jnp.concatenate(
                [jnp.sum(prod[:64], axis=0, keepdims=True), jnp.sum(prod[64:], axis=0, keepdims=True)], axis=1
            )
            acc[1] += lax.dot_general(pb, bdo, NT, preferred_element_type=F32)
            ds = (probs * (dpr - delta)).astype(BF16)
            acc[0] += lax.dot_general(ds, bdq, NT, preferred_element_type=F32)
            dq = fold_diag(jnp.dot(k_t[...], ds, preferred_element_type=F32)) * 0.125
            gbuf[c, 0, lanes, :] = dq.T.astype(BF16)

        gbuf[c, 1] = acc[0].astype(BF16)
        gbuf[c, 2] = acc[1].astype(BF16)
        for d in (2, 1, 3):
            ret_copy(c, d).start()
        ret_own(c).start()

    def relay(d):
        z_copy(d).wait_recv()
        y_copy(d).start()
        c_copy(d).start()

    def quarter(d):
        c_copy(d).wait_recv()
        f_copy(d).wait_recv()
        b = lax.rem(me_b - d + branch, branch)
        pieces = []
        for j in range(seq):
            block = slots[b * seq + j].astype(F32)
            pieces += [block[:, i * model:(i + 1) * model] for i in range(full)]
            rest = block[:, full * model:]
            pieces.append(jnp.concatenate([rest[:8], rest[8:, :model - half]], axis=1))
        pieces.append(jnp.zeros((up.shape[1] - part, model), F32))
        up[b] = jnp.concatenate(pieces, axis=0).astype(BF16)
        at = pl.ds(pl.multiple_of(b * part, 16), part)
        grad_s[at, :] = factor * lax.dot_general(up[b, :part, :], w_ref[...], NT, preferred_element_type=F32)

    def turn(d):
        b = lax.rem(me_b - d + branch, branch)
        group = up.shape[1]
        up_t[:, pl.ds(pl.multiple_of(b * group, W), group)] = up[b].T

    def weight(c):
        att = att_t[c]
        fill = jnp.zeros((W, up.shape[1] - part), BF16)
        pieces = []
        for b in range(branch):
            pieces += [att[:, b * part:(b + 1) * part], fill]
        att = jnp.concatenate(pieces, axis=1)
        sum_ = lax.dot_general(up_t[...], att, NT, preferred_element_type=F32)
        partf[c] = sum_ * factor
        for d in range(1, dp):
            to = lax.rem(me_dp + d, dp)
            part_b[d - 1, c] = partf[c, pl.ds(pl.multiple_of(to * share, 8), share), :].astype(BF16)
            dp_copy(c, d).start()

    share = wg_ref.shape[0]
    def cross(d):
        y_copy(d).wait_recv()
        f_copy(d).start()

    y_copy(0).wait_recv()
    f_copy(0).start()
    b_copy(1).start()
    b_copy(branch - 1).start()
    relay(1)
    z_copy(2).start()
    relay(branch - 1)
    b_copy(1).wait_recv()
    b_copy(2).start()
    quarter(0)
    turn(0)
    cross(1)
    relay(2)
    send_qkv(1)
    b_copy(branch - 1).wait_recv()
    cross(branch - 1)
    quarter(1)
    turn(1)
    b_copy(2).wait_recv()
    cross(2)
    quarter(branch - 1)
    turn(branch - 1)
    quarter(2)
    turn(2)

    def head_pair(c, carry):
        attention(c)
        weight(c)
        return carry

    lax.fori_loop(0, chunks, head_pair, 0)

    for c in range(chunks):
        total = partf[c, pl.ds(pl.multiple_of(me_dp * share, 8), share), :]
        for d in range(1, dp):
            dp_copy(c, d).wait_recv()
            total = total + rbuf[d - 1, c].astype(F32)
        wg_ref[:, c * W:(c + 1) * W] = total

    for c in range(chunks):
        ret_own(c).wait()
        for d in range(1, seq):
            ret_copy(c, d).wait_recv()
            ret_copy(c, d).wait_send()
            qkv_copy(c, d).wait_send()
    for d in range(1, branch):
        z_copy(d).wait_send()
        b_copy(d).wait_send()
    for d in range(branch):
        y_copy(d).wait_send()
        c_copy(d).wait_send()
        f_copy(d).wait_send()
    for d in range(1, dp):
        for c in range(chunks):
            dp_copy(c, d).wait_send()


def body(dp, seq, branch, qkv, grad_base, w_out, scale_level, text_count):
    part, _, features = qkv.shape[2:]
    tokens = part * seq
    width = features // seq
    chunks = width // W
    rows, model = grad_base.shape[1:]
    tiles = rows // 8 * (model // W)
    packed = (tiles + tiles % 2) // 2 * W
    group = -(-part // W) * W
    share = model // dp
    dma = pltpu.SemaphoreType.DMA
    vm = pltpu.VMEM
    vspec = pl.BlockSpec(memory_space=pltpu.VMEM)
    sspec = pl.BlockSpec(memory_space=pltpu.SMEM)
    anyspec = pl.BlockSpec(memory_space=pl.ANY)
    grads, weight_grad = pl.pallas_call(
        functools.partial(kernel, dp, seq, branch, chunks, tokens),
        out_shape=(
            jax.ShapeDtypeStruct((3, part, features), BF16),
            jax.ShapeDtypeStruct((share, width), F32),
        ),
        in_specs=[anyspec, vspec, vspec, sspec, sspec],
        out_specs=(anyspec, vspec),
        scratch_shapes=[
            vm((chunks, 3, tokens, W), BF16),
            vm((branch * seq, 16, packed), BF16),
            vm((branch, group, model), BF16),
            vm((model, branch * group), BF16),
            vm((tokens, width), F32),
            vm((W, tokens), BF16),
            vm((chunks, W, tokens), BF16),
            vm((W, tokens), BF16),
            vm((W, tokens), BF16),
            vm((W, tokens), BF16),
            vm((chunks, 3, tokens, W), BF16),
            vm((2, tokens, W), F32),
            vm((chunks, model, W), F32),
            vm((dp - 1, chunks, share, W), BF16),
            vm((dp - 1, chunks, share, W), BF16),
            dma((chunks, seq - 1)), dma((chunks, seq - 1)),
            dma((chunks, seq - 1)), dma((chunks, seq - 1)),
            dma((branch - 1,)), dma((branch - 1,)),
            dma((branch - 1,)), dma((branch - 1,)),
            dma((branch,)), dma((branch,)),
            dma((branch,)), dma((branch,)),
            dma((branch,)), dma((branch,)),
            dma((dp - 1, chunks)), dma((dp - 1, chunks)),
            dma((chunks,)), dma((chunks,)),
        ],
        compiler_params=pltpu.CompilerParams(
            collective_id=0, has_side_effects=True, vmem_limit_bytes=58 * 1024 * 1024
        ),
    )(jnp.transpose(qkv[0, 0], (1, 0, 2)), grad_base[0], w_out[0], scale_level, text_count)
    return (jnp.transpose(grads, (1, 0, 2))[None, None], weight_grad[None])


def solution(mesh):
    sizes = mesh.shape
    in_specs = (
        P("branch", "dp", "seq", None, None),
        P("dp", ("branch", "seq"), None),
        P("branch", "seq", None),
        P("dp"),
        P("dp"),
    )
    out_specs = (P("branch", "dp", "seq", None, None), P("branch", "dp", "seq"))
    run = functools.partial(body, sizes["dp"], sizes["seq"], sizes["branch"])
    return jax.shard_map(run, mesh=mesh, in_specs=in_specs, out_specs=out_specs, check_vma=False)
```

```python
import functools

import jax
import jax.numpy as jnp
from jax import lax
from jax.experimental import pallas as pl
from jax.experimental.pallas import tpu as pltpu
from jax.sharding import PartitionSpec as P

LAT = 512
MIN_TEXT = 96
F32 = jnp.float32
BF16 = jnp.bfloat16
MESH = pl.DeviceIdType.MESH
NT = (((1,), (1,)), ((), ()))
W = 128


def block_diag(pair):
    row = lax.broadcasted_iota(jnp.int32, pair.shape, 0)
    top = row < 64
    zero = jnp.zeros_like(pair)
    return jnp.concatenate([jnp.where(top, pair, zero), jnp.where(top, zero, pair)], axis=1)


def fold_diag(wide):
    row = lax.broadcasted_iota(jnp.int32, (wide.shape[0], W), 0)
    return jnp.where(row < 64, wide[:, :W], wide[:, W:])


def kernel(
    dp, seq, branch, chunks, tokens,
    x_ref, gb_ref, w_ref, level_ref, count_ref,
    out_ref, wg_ref,
    inb, slots, up, up_t, grad_s, do_t, probs_s, o_s, q_t, k_t, v_t, gbuf, acc, partf, part_b, rbuf,
    qs, qr, rs, rr, zs, zr, bs, br, ys, yr, cs, cr, fs, fr, ds_, dr, own_q, own_r,
):
    me_dp = lax.axis_index("dp")
    me_b = lax.axis_index("branch")
    me = lax.axis_index("seq")
    part = tokens // seq
    width = chunks * W
    nblk = tokens // W
    across = lax.rem(me + 2, seq)
    beside = me + 1 - 2 * lax.rem(me, 2)

    barrier = pltpu.get_barrier_semaphore()
    for d in range(1, branch):
        pl.semaphore_signal(barrier, inc=1, device_id={"branch": lax.rem(me_b + d, branch)}, device_id_type=MESH)
    for d in range(1, seq):
        pl.semaphore_signal(barrier, inc=1, device_id={"seq": lax.rem(me + d, seq)}, device_id_type=MESH)
    for d in range(1, dp):
        pl.semaphore_signal(barrier, inc=1, device_id={"dp": lax.rem(me_dp + d, dp)}, device_id_type=MESH)

    own = me_b * seq + me
    rows, model = gb_ref.shape
    full = rows // 16
    half = (slots.shape[2] - full * model)
    last = gb_ref[...].astype(F32)[full * 16:]
    filler = jnp.zeros((8, 2 * half - model), F32)
    last = jnp.concatenate([last[:, :half], jnp.concatenate([last[:, half:], filler], axis=1)], axis=0)
    for i in range(full):
        slots[own, :, i * model:(i + 1) * model] = gb_ref[i * 16:(i + 1) * 16, :]
    slots[own, :, full * model:] = last.astype(BF16)
    pl.semaphore_wait(barrier, branch + seq + dp - 3)

    def remote(src, dst, ssem, rsem, axis, index):
        return pltpu.make_async_remote_copy(
            src_ref=src, dst_ref=dst, send_sem=ssem, recv_sem=rsem,
            device_id={axis: index}, device_id_type=MESH,
        )

    def qkv_copy(c, d):
        to = lax.rem(me + d, seq)
        lanes = pl.ds(pl.multiple_of(to * width + c * W, W), W)
        at = pl.ds(pl.multiple_of(me * part, 16), part)
        return remote(x_ref.at[:, :, lanes], inb.at[c, :, at, :], qs.at[c, d - 1], qr.at[c, d - 1], "seq", to)

    def qkv_own(c):
        lanes = pl.ds(pl.multiple_of(me * width + c * W, W), W)
        at = pl.ds(pl.multiple_of(me * part, 16), part)
        return pltpu.make_async_copy(x_ref.at[:, :, lanes], inb.at[c, :, at, :], own_q.at[c])

    def line(d):
        return lax.rem(me_b - d + branch, branch) * seq + me

    cut = slots.shape[2] // W // 2 * W
    first, second = slice(0, cut), slice(cut, slots.shape[2])

    def on_line(d):
        if d in (1, branch - 1):
            return 0, lax.rem(me_b + d, branch)
        return d - 1, lax.rem(me_b + 1, branch)

    def z_copy(d):
        back, to = on_line(d)
        block = slots.at[line(back)]
        return remote(block, block, zs.at[d - 1], zr.at[d - 1], "branch", to)

    def b_copy(d):
        back, to = on_line(d)
        k = lax.rem(me_b - back + branch, branch) * seq + across
        block = slots.at[k, :, second]
        return remote(block, block, bs.at[d - 1], br.at[d - 1], "branch", to)

    def y_copy(d):
        block = slots.at[line(d)] if d == 0 else slots.at[line(d), :, first]
        return remote(block, block, ys.at[d], yr.at[d], "seq", across)

    def c_copy(d):
        return remote(slots.at[line(d)], slots.at[line(d)], cs.at[d], cr.at[d], "seq", beside)

    def f_copy(d):
        k = lax.rem(me_b - d + branch, branch) * seq + across
        return remote(slots.at[k], slots.at[k], fs.at[d], fr.at[d], "seq", beside)

    def ret_copy(c, d):
        to = lax.rem(me + d, seq)
        lanes = pl.ds(pl.multiple_of(me * width + c * W, W), W)
        at = pl.ds(pl.multiple_of(to * part, 16), part)
        return remote(gbuf.at[c, :, at, :], out_ref.at[:, :, lanes], rs.at[c, d - 1], rr.at[c, d - 1], "seq", to)

    def ret_own(c):
        lanes = pl.ds(pl.multiple_of(me * width + c * W, W), W)
        at = pl.ds(pl.multiple_of(me * part, 16), part)
        return pltpu.make_async_copy(gbuf.at[c, :, at, :], out_ref.at[:, :, lanes], own_r.at[c])

    def dp_copy(c, d):
        to = lax.rem(me_dp + d, dp)
        return remote(part_b.at[d - 1, c], rbuf.at[d - 1, c], ds_.at[d - 1, c], dr.at[d - 1, c], "dp", to)

    def send_qkv(c):
        for d in (2, 1, 3):
            qkv_copy(c, d).start()
        qkv_own(c).start()

    z_copy(1).start()
    z_copy(branch - 1).start()
    y_copy(0).start()
    c_copy(0).start()
    send_qkv(0)
    send_qkv(1)

    level = level_ref[0]
    limit = LAT + count_ref[0]
    factor = jnp.where(me_b == 0, jnp.float32(1.0), (level + 2 * me_b).astype(F32) / 8.0)
    safe = LAT + MIN_TEXT
    tail = safe + lax.broadcasted_iota(jnp.int32, (tokens - safe, 2 * W), 0)

    def forward(c):
        for d in range(1, seq):
            qkv_copy(c, d).wait_recv()
        qkv_own(c).wait()
        q_t[c] = (inb[c, 0].astype(F32) * 0.125).T.astype(BF16)
        k_t[c] = inb[c, 1].astype(F32).T.astype(BF16)
        v_t[c] = inb[c, 2].astype(F32).T.astype(BF16)

        def step(i, carry):
            lanes = pl.ds(pl.multiple_of(i * W, W), W)
            wide = pl.ds(pl.multiple_of(i * 2 * W, 2 * W), 2 * W)
            s = jnp.dot(inb[c, 1], block_diag(q_t[c, :, lanes]), preferred_element_type=F32)
            s = jnp.concatenate([s[:safe], jnp.where(tail < limit, s[safe:], -1e30)], axis=0)
            e = jnp.exp(s - jnp.max(s, axis=0, keepdims=True))
            pb = (e * (1.0 / jnp.sum(e, axis=0, keepdims=True))).astype(BF16)
            probs_s[c, :, wide] = pb
            o_s[c, :, lanes] = fold_diag(jnp.dot(v_t[c], pb, preferred_element_type=F32))
            return carry

        lax.fori_loop(0, nblk, step, 0)

    def backward(c):
        do_t[...] = grad_s[:, pl.ds(pl.multiple_of(c * W, W), W)].T.astype(BF16)
        acc[...] = jnp.zeros_like(acc)
        for i in range(nblk):
            lanes = slice(i * W, (i + 1) * W)
            do = do_t[:, lanes]
            bdo = block_diag(do)
            dpr = jnp.dot(inb[c, 2], bdo, preferred_element_type=F32)
            prod = do.astype(F32) * o_s[c, :, lanes]
            delta = jnp.concatenate(
                [jnp.sum(prod[:64], axis=0, keepdims=True), jnp.sum(prod[64:], axis=0, keepdims=True)], axis=1
            )
            pb = probs_s[c, :, 2 * i * W:2 * (i + 1) * W]
            acc[1] += lax.dot_general(pb, bdo, NT, preferred_element_type=F32)
            ds = (pb.astype(F32) * (dpr - delta)).astype(BF16)
            acc[0] += lax.dot_general(ds, block_diag(q_t[c, :, lanes]), NT, preferred_element_type=F32)
            dq = fold_diag(jnp.dot(k_t[c], ds, preferred_element_type=F32)) * 0.125
            gbuf[c, 0, lanes, :] = dq.T.astype(BF16)

        gbuf[c, 1] = acc[0].astype(BF16)
        gbuf[c, 2] = acc[1].astype(BF16)
        for d in (2, 1, 3):
            ret_copy(c, d).start()
        ret_own(c).start()

    def relay(d):
        z_copy(d).wait_recv()
        y_copy(d).start()
        c_copy(d).start()

    def quarter(d):
        c_copy(d).wait_recv()
        f_copy(d).wait_recv()
        b = lax.rem(me_b - d + branch, branch)
        pieces = []
        for j in range(seq):
            block = slots[b * seq + j].astype(F32)
            pieces += [block[:, i * model:(i + 1) * model] for i in range(full)]
            rest = block[:, full * model:]
            pieces.append(jnp.concatenate([rest[:8], rest[8:, :model - half]], axis=1))
        pieces.append(jnp.zeros((up.shape[1] - part, model), F32))
        up[b] = jnp.concatenate(pieces, axis=0).astype(BF16)
        at = pl.ds(pl.multiple_of(b * part, 16), part)
        grad_s[at, :] = factor * lax.dot_general(up[b, :part, :], w_ref[...], NT, preferred_element_type=F32)

    def turn(d):
        b = lax.rem(me_b - d + branch, branch)
        group = up.shape[1]
        up_t[:, pl.ds(pl.multiple_of(b * group, W), group)] = up[b].T

    def weight(c):
        att = o_s[c].astype(BF16)
        fill = jnp.zeros((W, up.shape[1] - part), BF16)
        pieces = []
        for b in range(branch):
            pieces += [att[:, b * part:(b + 1) * part], fill]
        att = jnp.concatenate(pieces, axis=1)
        sum_ = lax.dot_general(up_t[...], att, NT, preferred_element_type=F32)
        partf[c] = sum_ * factor
        for d in range(1, dp):
            to = lax.rem(me_dp + d, dp)
            part_b[d - 1, c] = partf[c, pl.ds(pl.multiple_of(to * share, 8), share), :].astype(BF16)
            dp_copy(c, d).start()

    share = wg_ref.shape[0]
    def cross(d):
        y_copy(d).wait_recv()
        f_copy(d).start()

    y_copy(0).wait_recv()
    f_copy(0).start()
    b_copy(1).start()
    b_copy(branch - 1).start()
    relay(1)
    z_copy(2).start()
    relay(branch - 1)
    b_copy(1).wait_recv()
    b_copy(2).start()
    forward(0)
    cross(1)
    relay(2)
    for c in range(2, chunks):
        send_qkv(c)
    quarter(0)
    turn(0)
    b_copy(branch - 1).wait_recv()
    cross(branch - 1)
    quarter(1)
    forward(1)
    b_copy(2).wait_recv()
    cross(2)
    turn(1)
    quarter(branch - 1)
    turn(branch - 1)
    for c in range(2, chunks):
        forward(c)
    quarter(2)
    turn(2)

    def head_pair(c, carry):
        weight(c)
        backward(c)
        return carry

    lax.fori_loop(0, chunks, head_pair, 0)

    for c in range(chunks):
        total = partf[c, pl.ds(pl.multiple_of(me_dp * share, 8), share), :]
        for d in range(1, dp):
            dp_copy(c, d).wait_recv()
            total = total + rbuf[d - 1, c].astype(F32)
        wg_ref[:, c * W:(c + 1) * W] = total

    for c in range(chunks):
        ret_own(c).wait()
        for d in range(1, seq):
            ret_copy(c, d).wait_recv()
            ret_copy(c, d).wait_send()
            qkv_copy(c, d).wait_send()
    for d in range(1, branch):
        z_copy(d).wait_send()
        b_copy(d).wait_send()
    for d in range(branch):
        y_copy(d).wait_send()
        c_copy(d).wait_send()
        f_copy(d).wait_send()
    for d in range(1, dp):
        for c in range(chunks):
            dp_copy(c, d).wait_send()


def hand_over(grads_ref, weight_ref, grads_out, weight_out, grads_v, weight_v, in_sem, out_sem):
    moves = [(grads_ref.at[i], grads_v.at[i], grads_out.at[i]) for i in range(3)]
    moves.append((weight_ref, weight_v, weight_out))
    loads = [pltpu.make_async_copy(a, v, in_sem.at[i]) for i, (a, v, _) in enumerate(moves)]
    stores = [pltpu.make_async_copy(v, b, out_sem.at[i]) for i, (_, v, b) in enumerate(moves)]
    for load in loads:
        load.start()
    for load, store in zip(loads, stores):
        load.wait()
        store.start()
    for store in stores:
        store.wait()


def body(dp, seq, branch, qkv, grad_base, w_out, scale_level, text_count):
    part, _, features = qkv.shape[2:]
    tokens = part * seq
    width = features // seq
    chunks = width // W
    rows, model = grad_base.shape[1:]
    tiles = rows // 8 * (model // W)
    packed = (tiles + tiles % 2) // 2 * W
    group = -(-part // W) * W
    share = model // dp
    dma = pltpu.SemaphoreType.DMA
    vm = pltpu.VMEM
    vspec = pl.BlockSpec(memory_space=pltpu.VMEM)
    sspec = pl.BlockSpec(memory_space=pltpu.SMEM)
    anyspec = pl.BlockSpec(memory_space=pl.ANY)
    grads, weight_grad = pl.pallas_call(
        functools.partial(kernel, dp, seq, branch, chunks, tokens),
        out_shape=(
            jax.ShapeDtypeStruct((3, part, features), BF16),
            jax.ShapeDtypeStruct((share, width), F32),
        ),
        in_specs=[anyspec, vspec, vspec, sspec, sspec],
        out_specs=(anyspec, vspec),
        scratch_shapes=[
            vm((chunks, 3, tokens, W), BF16),
            vm((branch * seq, 16, packed), BF16),
            vm((branch, group, model), BF16),
            vm((model, branch * group), BF16),
            vm((tokens, width), F32),
            vm((W, tokens), BF16),
            vm((chunks, tokens, 2 * tokens), BF16),
            vm((chunks, W, tokens), F32),
            vm((chunks, W, tokens), BF16),
            vm((chunks, W, tokens), BF16),
            vm((chunks, W, tokens), BF16),
            vm((chunks, 3, tokens, W), BF16),
            vm((2, tokens, W), F32),
            vm((chunks, model, W), F32),
            vm((dp - 1, chunks, share, W), BF16),
            vm((dp - 1, chunks, share, W), BF16),
            dma((chunks, seq - 1)), dma((chunks, seq - 1)),
            dma((chunks, seq - 1)), dma((chunks, seq - 1)),
            dma((branch - 1,)), dma((branch - 1,)),
            dma((branch - 1,)), dma((branch - 1,)),
            dma((branch,)), dma((branch,)),
            dma((branch,)), dma((branch,)),
            dma((branch,)), dma((branch,)),
            dma((dp - 1, chunks)), dma((dp - 1, chunks)),
            dma((chunks,)), dma((chunks,)),
        ],
        compiler_params=pltpu.CompilerParams(
            collective_id=0, has_side_effects=True, vmem_limit_bytes=58 * 1024 * 1024
        ),
    )(jnp.transpose(qkv[0, 0], (1, 0, 2)), grad_base[0], w_out[0], scale_level, text_count)
    grads, weight_grad = pl.pallas_call(
        hand_over,
        out_shape=(
            jax.ShapeDtypeStruct(grads.shape, BF16),
            jax.ShapeDtypeStruct(weight_grad.shape, F32),
        ),
        in_specs=[anyspec, anyspec],
        out_specs=(anyspec, anyspec),
        scratch_shapes=[vm(grads.shape, BF16), vm(weight_grad.shape, F32), dma((4,)), dma((4,))],
        compiler_params=pltpu.CompilerParams(vmem_limit_bytes=58 * 1024 * 1024),
    )(grads, weight_grad)
    return (jnp.transpose(grads, (1, 0, 2))[None, None], weight_grad[None])


def solution(mesh):
    sizes = mesh.shape
    in_specs = (
        P("branch", "dp", "seq", None, None),
        P("dp", ("branch", "seq"), None),
        P("branch", "seq", None),
        P("dp"),
        P("dp"),
    )
    out_specs = (P("branch", "dp", "seq", None, None), P("branch", "dp", "seq"))
    run = functools.partial(body, sizes["dp"], sizes["seq"], sizes["branch"])
    return jax.shard_map(run, mesh=mesh, in_specs=in_specs, out_specs=out_specs, check_vma=False)
```

```python
import functools

import jax
import jax.numpy as jnp
from jax import lax
from jax.experimental import pallas as pl
from jax.experimental.pallas import tpu as pltpu
from jax.sharding import PartitionSpec as P

LAT = 512
MIN_TEXT = 96
F32 = jnp.float32
BF16 = jnp.bfloat16
MESH = pl.DeviceIdType.MESH
NT = (((1,), (1,)), ((), ()))
W = 128


def block_diag(pair):
    row = lax.broadcasted_iota(jnp.int32, pair.shape, 0)
    top = row < 64
    zero = jnp.zeros_like(pair)
    return jnp.concatenate([jnp.where(top, pair, zero), jnp.where(top, zero, pair)], axis=1)


def fold_diag(wide):
    row = lax.broadcasted_iota(jnp.int32, (wide.shape[0], W), 0)
    return jnp.where(row < 64, wide[:, :W], wide[:, W:])


def kernel(
    dp, seq, branch, chunks, tokens,
    x_ref, gb_ref, w_ref, level_ref, count_ref,
    out_ref, wg_ref,
    inb, slots, up, up_t, grad_s, do_t, att_t, q_t, k_t, v_t, gbuf, acc, partf, part_b, rbuf,
    qs, qr, rs, rr, zs, zr, bs, br, ys, yr, cs, cr, fs, fr, ds_, dr, own_q, own_r,
):
    me_dp = lax.axis_index("dp")
    me_b = lax.axis_index("branch")
    me = lax.axis_index("seq")
    part = tokens // seq
    width = chunks * W
    nblk = tokens // W
    across = lax.rem(me + 2, seq)
    beside = me + 1 - 2 * lax.rem(me, 2)

    barrier = pltpu.get_barrier_semaphore()
    for d in range(1, branch):
        pl.semaphore_signal(barrier, inc=1, device_id={"branch": lax.rem(me_b + d, branch)}, device_id_type=MESH)
    for d in range(1, seq):
        pl.semaphore_signal(barrier, inc=1, device_id={"seq": lax.rem(me + d, seq)}, device_id_type=MESH)
    for d in range(1, dp):
        pl.semaphore_signal(barrier, inc=1, device_id={"dp": lax.rem(me_dp + d, dp)}, device_id_type=MESH)

    own = me_b * seq + me
    rows, model = gb_ref.shape
    full = rows // 16
    half = (slots.shape[2] - full * model)
    last = gb_ref[...].astype(F32)[full * 16:]
    filler = jnp.zeros((8, 2 * half - model), F32)
    last = jnp.concatenate([last[:, :half], jnp.concatenate([last[:, half:], filler], axis=1)], axis=0)
    for i in range(full):
        slots[own, :, i * model:(i + 1) * model] = gb_ref[i * 16:(i + 1) * 16, :]
    slots[own, :, full * model:] = last.astype(BF16)
    pl.semaphore_wait(barrier, branch + seq + dp - 3)

    def remote(src, dst, ssem, rsem, axis, index):
        return pltpu.make_async_remote_copy(
            src_ref=src, dst_ref=dst, send_sem=ssem, recv_sem=rsem,
            device_id={axis: index}, device_id_type=MESH,
        )

    def qkv_copy(c, d):
        to = lax.rem(me + d, seq)
        lanes = pl.ds(pl.multiple_of(to * width + c * W, W), W)
        at = pl.ds(pl.multiple_of(me * part, 16), part)
        return remote(x_ref.at[:, :, lanes], inb.at[c, :, at, :], qs.at[c, d - 1], qr.at[c, d - 1], "seq", to)

    def qkv_own(c):
        lanes = pl.ds(pl.multiple_of(me * width + c * W, W), W)
        at = pl.ds(pl.multiple_of(me * part, 16), part)
        return pltpu.make_async_copy(x_ref.at[:, :, lanes], inb.at[c, :, at, :], own_q.at[c])

    def line(d):
        return lax.rem(me_b - d + branch, branch) * seq + me

    cut = slots.shape[2] // W // 2 * W
    first, second = slice(0, cut), slice(cut, slots.shape[2])

    def on_line(d):
        if d in (1, branch - 1):
            return 0, lax.rem(me_b + d, branch)
        return d - 1, lax.rem(me_b + 1, branch)

    def z_copy(d):
        back, to = on_line(d)
        block = slots.at[line(back)]
        return remote(block, block, zs.at[d - 1], zr.at[d - 1], "branch", to)

    def b_copy(d):
        back, to = on_line(d)
        k = lax.rem(me_b - back + branch, branch) * seq + across
        block = slots.at[k, :, second]
        return remote(block, block, bs.at[d - 1], br.at[d - 1], "branch", to)

    def y_copy(d):
        block = slots.at[line(d)] if d == 0 else slots.at[line(d), :, first]
        return remote(block, block, ys.at[d], yr.at[d], "seq", across)

    def c_copy(d):
        return remote(slots.at[line(d)], slots.at[line(d)], cs.at[d], cr.at[d], "seq", beside)

    def f_copy(d):
        k = lax.rem(me_b - d + branch, branch) * seq + across
        return remote(slots.at[k], slots.at[k], fs.at[d], fr.at[d], "seq", beside)

    def ret_copy(c, d):
        to = lax.rem(me + d, seq)
        lanes = pl.ds(pl.multiple_of(me * width + c * W, W), W)
        at = pl.ds(pl.multiple_of(to * part, 16), part)
        return remote(gbuf.at[c, :, at, :], out_ref.at[:, :, lanes], rs.at[c, d - 1], rr.at[c, d - 1], "seq", to)

    def ret_own(c):
        lanes = pl.ds(pl.multiple_of(me * width + c * W, W), W)
        at = pl.ds(pl.multiple_of(me * part, 16), part)
        return pltpu.make_async_copy(gbuf.at[c, :, at, :], out_ref.at[:, :, lanes], own_r.at[c])

    def dp_copy(c, d):
        to = lax.rem(me_dp + d, dp)
        return remote(part_b.at[d - 1, c], rbuf.at[d - 1, c], ds_.at[d - 1, c], dr.at[d - 1, c], "dp", to)

    def send_qkv(c):
        for d in (2, 1, 3):
            qkv_copy(c, d).start()
        qkv_own(c).start()

    z_copy(1).start()
    z_copy(branch - 1).start()
    y_copy(0).start()
    c_copy(0).start()
    send_qkv(0)

    level = level_ref[0]
    limit = LAT + count_ref[0]
    factor = jnp.where(me_b == 0, jnp.float32(1.0), (level + 2 * me_b).astype(F32) / 8.0)
    safe = LAT + MIN_TEXT
    tail = safe + lax.broadcasted_iota(jnp.int32, (tokens - safe, 2 * W), 0)

    def attention(c):
        for d in range(1, seq):
            qkv_copy(c, d).wait_recv()
        qkv_own(c).wait()

        @pl.when(c + 2 < chunks)
        def _():
            send_qkv(c + 2)

        q_t[...] = (inb[c, 0].astype(F32) * 0.125).T.astype(BF16)
        k_t[...] = inb[c, 1].astype(F32).T.astype(BF16)
        v_t[...] = inb[c, 2].astype(F32).T.astype(BF16)
        do_t[...] = grad_s[:, pl.ds(pl.multiple_of(c * W, W), W)].T.astype(BF16)
        acc[...] = jnp.zeros_like(acc)

        for i in range(nblk):
            lanes = slice(i * W, (i + 1) * W)
            do = do_t[:, lanes]
            bdq = block_diag(q_t[:, lanes])
            bdo = block_diag(do)
            s = jnp.dot(inb[c, 1], bdq, preferred_element_type=F32)
            dpr = jnp.dot(inb[c, 2], bdo, preferred_element_type=F32)
            s = jnp.concatenate([s[:safe], jnp.where(tail < limit, s[safe:], -1e30)], axis=0)
            e = jnp.exp(s - jnp.max(s, axis=0, keepdims=True))
            probs = e * (1.0 / jnp.sum(e, axis=0, keepdims=True))
            pb = probs.astype(BF16)
            o = fold_diag(jnp.dot(v_t[...], pb, preferred_element_type=F32))
            att_t[c, :, lanes] = o.astype(BF16)
            prod = do.astype(F32) * o
            delta = jnp.concatenate(
                [jnp.sum(prod[:64], axis=0, keepdims=True), jnp.sum(prod[64:], axis=0, keepdims=True)], axis=1
            )
            acc[1] += lax.dot_general(pb, bdo, NT, preferred_element_type=F32)
            ds = (probs * (dpr - delta)).astype(BF16)
            acc[0] += lax.dot_general(ds, bdq, NT, preferred_element_type=F32)
            dq = fold_diag(jnp.dot(k_t[...], ds, preferred_element_type=F32)) * 0.125
            gbuf[c, 0, lanes, :] = dq.T.astype(BF16)

        gbuf[c, 1] = acc[0].astype(BF16)
        gbuf[c, 2] = acc[1].astype(BF16)
        for d in (2, 1, 3):
            ret_copy(c, d).start()
        ret_own(c).start()

    def relay(d):
        z_copy(d).wait_recv()
        y_copy(d).start()
        c_copy(d).start()

    def quarter(d):
        c_copy(d).wait_recv()
        f_copy(d).wait_recv()
        b = lax.rem(me_b - d + branch, branch)
        pieces = []
        for j in range(seq):
            block = slots[b * seq + j].astype(F32)
            pieces += [block[:, i * model:(i + 1) * model] for i in range(full)]
            rest = block[:, full * model:]
            pieces.append(jnp.concatenate([rest[:8], rest[8:, :model - half]], axis=1))
        pieces.append(jnp.zeros((up.shape[1] - part, model), F32))
        up[b] = jnp.concatenate(pieces, axis=0).astype(BF16)
        at = pl.ds(pl.multiple_of(b * part, 16), part)
        grad_s[at, :] = factor * lax.dot_general(up[b, :part, :], w_ref[...], NT, preferred_element_type=F32)

    def turn(d):
        b = lax.rem(me_b - d + branch, branch)
        group = up.shape[1]
        up_t[:, pl.ds(pl.multiple_of(b * group, W), group)] = up[b].T

    def weight(c):
        att = att_t[c]
        fill = jnp.zeros((W, up.shape[1] - part), BF16)
        pieces = []
        for b in range(branch):
            pieces += [att[:, b * part:(b + 1) * part], fill]
        att = jnp.concatenate(pieces, axis=1)
        sum_ = lax.dot_general(up_t[...], att, NT, preferred_element_type=F32)
        partf[c] = sum_ * factor
        for d in range(1, dp):
            to = lax.rem(me_dp + d, dp)
            part_b[d - 1, c] = partf[c, pl.ds(pl.multiple_of(to * share, 8), share), :].astype(BF16)
            dp_copy(c, d).start()

    share = wg_ref.shape[0]
    def cross(d):
        y_copy(d).wait_recv()
        f_copy(d).start()

    y_copy(0).wait_recv()
    f_copy(0).start()
    b_copy(1).start()
    b_copy(branch - 1).start()
    relay(1)
    z_copy(2).start()
    relay(branch - 1)
    b_copy(1).wait_recv()
    b_copy(2).start()
    quarter(0)
    turn(0)
    cross(1)
    relay(2)
    send_qkv(1)
    b_copy(branch - 1).wait_recv()
    cross(branch - 1)
    quarter(1)
    turn(1)
    b_copy(2).wait_recv()
    cross(2)
    quarter(branch - 1)
    turn(branch - 1)
    quarter(2)
    turn(2)

    def head_pair(c, carry):
        attention(c)
        weight(c)
        return carry

    lax.fori_loop(0, chunks, head_pair, 0)

    for c in range(chunks):
        total = partf[c, pl.ds(pl.multiple_of(me_dp * share, 8), share), :]
        for d in range(1, dp):
            dp_copy(c, d).wait_recv()
            total = total + rbuf[d - 1, c].astype(F32)
        wg_ref[:, c * W:(c + 1) * W] = total

    for c in range(chunks):
        ret_own(c).wait()
        for d in range(1, seq):
            ret_copy(c, d).wait_recv()
            ret_copy(c, d).wait_send()
            qkv_copy(c, d).wait_send()
    for d in range(1, branch):
        z_copy(d).wait_send()
        b_copy(d).wait_send()
    for d in range(branch):
        y_copy(d).wait_send()
        c_copy(d).wait_send()
        f_copy(d).wait_send()
    for d in range(1, dp):
        for c in range(chunks):
            dp_copy(c, d).wait_send()


def hand_over(grads_ref, weight_ref, grads_out, weight_out, grads_v, weight_v, in_sem, out_sem):
    moves = [(grads_ref.at[i], grads_v.at[i], grads_out.at[i]) for i in range(3)]
    moves.append((weight_ref, weight_v, weight_out))
    loads = [pltpu.make_async_copy(a, v, in_sem.at[i]) for i, (a, v, _) in enumerate(moves)]
    stores = [pltpu.make_async_copy(v, b, out_sem.at[i]) for i, (_, v, b) in enumerate(moves)]
    for load in loads:
        load.start()
    for load, store in zip(loads, stores):
        load.wait()
        store.start()
    for store in stores:
        store.wait()


def body(dp, seq, branch, qkv, grad_base, w_out, scale_level, text_count):
    part, _, features = qkv.shape[2:]
    tokens = part * seq
    width = features // seq
    chunks = width // W
    rows, model = grad_base.shape[1:]
    tiles = rows // 8 * (model // W)
    packed = (tiles + tiles % 2) // 2 * W
    group = -(-part // W) * W
    share = model // dp
    dma = pltpu.SemaphoreType.DMA
    vm = pltpu.VMEM
    vspec = pl.BlockSpec(memory_space=pltpu.VMEM)
    sspec = pl.BlockSpec(memory_space=pltpu.SMEM)
    anyspec = pl.BlockSpec(memory_space=pl.ANY)
    grads, weight_grad = pl.pallas_call(
        functools.partial(kernel, dp, seq, branch, chunks, tokens),
        out_shape=(
            jax.ShapeDtypeStruct((3, part, features), BF16),
            jax.ShapeDtypeStruct((share, width), F32),
        ),
        in_specs=[anyspec, vspec, vspec, sspec, sspec],
        out_specs=(anyspec, vspec),
        scratch_shapes=[
            vm((chunks, 3, tokens, W), BF16),
            vm((branch * seq, 16, packed), BF16),
            vm((branch, group, model), BF16),
            vm((model, branch * group), BF16),
            vm((tokens, width), F32),
            vm((W, tokens), BF16),
            vm((chunks, W, tokens), BF16),
            vm((W, tokens), BF16),
            vm((W, tokens), BF16),
            vm((W, tokens), BF16),
            vm((chunks, 3, tokens, W), BF16),
            vm((2, tokens, W), F32),
            vm((chunks, model, W), F32),
            vm((dp - 1, chunks, share, W), BF16),
            vm((dp - 1, chunks, share, W), BF16),
            dma((chunks, seq - 1)), dma((chunks, seq - 1)),
            dma((chunks, seq - 1)), dma((chunks, seq - 1)),
            dma((branch - 1,)), dma((branch - 1,)),
            dma((branch - 1,)), dma((branch - 1,)),
            dma((branch,)), dma((branch,)),
            dma((branch,)), dma((branch,)),
            dma((branch,)), dma((branch,)),
            dma((dp - 1, chunks)), dma((dp - 1, chunks)),
            dma((chunks,)), dma((chunks,)),
        ],
        compiler_params=pltpu.CompilerParams(
            collective_id=0, has_side_effects=True, vmem_limit_bytes=58 * 1024 * 1024
        ),
    )(jnp.transpose(qkv[0, 0], (1, 0, 2)), grad_base[0], w_out[0], scale_level, text_count)
    grads, weight_grad = pl.pallas_call(
        hand_over,
        out_shape=(
            jax.ShapeDtypeStruct(grads.shape, BF16),
            jax.ShapeDtypeStruct(weight_grad.shape, F32),
        ),
        in_specs=[anyspec, anyspec],
        out_specs=(anyspec, anyspec),
        scratch_shapes=[vm(grads.shape, BF16), vm(weight_grad.shape, F32), dma((4,)), dma((4,))],
        compiler_params=pltpu.CompilerParams(vmem_limit_bytes=58 * 1024 * 1024),
    )(grads, weight_grad)
    return (jnp.transpose(grads, (1, 0, 2))[None, None], weight_grad[None])


def solution(mesh):
    sizes = mesh.shape
    in_specs = (
        P("branch", "dp", "seq", None, None),
        P("dp", ("branch", "seq"), None),
        P("branch", "seq", None),
        P("dp"),
        P("dp"),
    )
    out_specs = (P("branch", "dp", "seq", None, None), P("branch", "dp", "seq"))
    run = functools.partial(body, sizes["dp"], sizes["seq"], sizes["branch"])
    return jax.shard_map(run, mesh=mesh, in_specs=in_specs, out_specs=out_specs, check_vma=False)
```
